32 devices in a mesh: groups: 2 (over y), wide: 4 (over z), narrow: 4 (over x, core).
Axes of the slice: x: 2, y: 2, z: 4, core: 2. Of those that a mesh axis runs over, the one named last changes fastest.
Arguments:
- tokens: bfloat16 [2, 128, 8192], P(None, ('groups', 'wide'), 'narrow'), parts along dimension 1, may hold values from -30 to 30
- assign: int32 [2, 128], P(None, 'groups'), parts along dimension 1, may hold values from 0 to 63, each once within a row
- state: bfloat16 [128, 2, 3, 8192], P(('groups', 'narrow'), None, None, 'wide'), parts along dimension 0, may hold values from -6 to 6
- norm_gain: float32 [8192], P('narrow'), may hold values from 0.1 to 1.9
- in_weight: bfloat16 [8192, 3, 8192], P('narrow', None, 'wide'), may hold values from -0.0625 to 0.0625
- conv_weight: float32 [3, 3, 8192], P(None, None, 'wide'), may hold values from -3 to 3
- out_weight: bfloat16 [8192, 8192], P('wide', 'narrow'), may hold values from -0.0625 to 0.0625
Outputs:
- mixer_out: bfloat16 [2, 128, 8192], P(None, ('groups', 'wide'), 'narrow'), parts along dimension 1
- new_state: bfloat16 [128, 2, 3, 8192], P(('groups', 'narrow'), None, None, 'wide'), parts along dimension 0
The draws below stay inside these ranges and needn't reach their ends.
There are 2 independent parts, one for each index of `groups`. The reference program is written for one: setup_inputs(seed, part) draws one part's arguments, and reference() takes and returns one part's arrays. A program takes and returns all parts, laid end to end along the dimension named above; an argument that names none is the same for every part. Nothing has to cross between parts.
Inputs may be any that keep to these rules, and one draw needn't show every extreme that they name: `assign`: each step's row is a permutation of the 64 candidates of the group.
All inputs are finite; a program needn't handle non-finite values.
Results may differ from the reference program's by a relative error of at most 0.019.
Values may be sent and summed in bfloat16 or wider, within the bound.
No kernel may reach another device: no remote copies, remote signals or barrier semaphores. Data moves between devices by JAX's collectives and lax.ppermute only.
A program may use at most 128 MiB of HBM per device.

```python
import math
import jax
import jax.numpy as jnp
from jax import lax

D = 8192
STEPS = 2
ROWS = 64
N_WIDE = 4
N_NARROW = 4


def draw_tokens(key, part):
    key = jax.random.fold_in(key, 11)
    first, second, third = jax.random.split(key, 3)
    columns = jnp.arange(D, dtype=jnp.float32) / D
    col_scale = jnp.exp(columns * math.log(3.0)) * jnp.exp(jax.random.uniform(second, (D,), jnp.float32, 0.0, math.log(10.0 / 3.0)))
    row_scale = jnp.exp(jax.random.uniform(third, (STEPS, ROWS, 1), jnp.float32, 0.0, math.log(10.0)))
    base = jax.random.normal(first, (STEPS, ROWS, D), jnp.float32)
    values = jnp.clip(base * col_scale * row_scale, -30.0, 30.0)
    return values.astype(jnp.bfloat16)


def steps_of(own_key, dims, cuts, low, high):
    loudness, own = 1.0, jax.random.fold_in(own_key, 6)
    for dim, shards_of in cuts:
        heights = jnp.exp(jax.random.uniform(jax.random.fold_in(own, dim), (shards_of,), jnp.float32, low / len(cuts), high / len(cuts)))
        loudness = loudness * jnp.repeat(heights, dims[dim] // shards_of).reshape([-1 if axis == dim else 1 for axis in range(len(dims))])
    return loudness


def bell_draw(own_key, extent, scale, reach, cuts=(), kind=jnp.bfloat16):
    factor_of = steps_of(own_key, extent, cuts, -0.22, 0.18) if cuts else 1.0
    array = jax.random.normal(own_key, extent, jnp.float32) * scale * factor_of
    return jnp.minimum(jnp.maximum(array, -reach), reach).astype(kind)


def setup_inputs(seed: int = 0, part: int = 0) -> dict:
    keys = jax.random.split(jax.random.key(seed), 8)
    own_keys = jax.random.split(jax.random.fold_in(keys[7], part), 8)
    return {
        "tokens": draw_tokens(jax.random.fold_in(jax.random.fold_in(keys[7], part), 71), part),
        "assign": jax.vmap(lambda own: jax.random.permutation(own, ROWS))(jax.random.split(own_keys[1], STEPS)).reshape((STEPS, ROWS)).astype(jnp.int32),
        "state": bell_draw(own_keys[2], (ROWS, 2, 3, D), 1.0, 6.0, ((0, 4), (3, 4))),
        "norm_gain": jnp.clip(1.0 + 0.18 * jax.random.normal(keys[3], (D,), jnp.float32), 0.1, 1.9),
        "in_weight": bell_draw(keys[4], (D, 3, D), D ** -0.5, 0.0625, ((0, 4), (2, 4))),
        "conv_weight": bell_draw(keys[5], (3, 3, D), 0.6, 3.0, ((2, 4),), jnp.float32),
        "out_weight": bell_draw(keys[6], (D, D), D ** -0.5, 0.0625, ((0, 4), (1, 4))),
    }


def block_sum(left, right, blocks):
    width = left.shape[1] // blocks

    def add_block(index, total):
        start = (index * width).astype(jnp.int32)
        piece = lax.dynamic_slice_in_dim(left, start, width, 1)
        weights = lax.dynamic_slice_in_dim(right, start, width, 0)
        term = jnp.dot(piece, weights, preferred_element_type=jnp.float32)
        rounded = lax.optimization_barrier(term.astype(jnp.bfloat16))
        return total + rounded.astype(jnp.float32)
    zeros = jnp.zeros((left.shape[0], right.shape[1]), jnp.float32)
    return lax.fori_loop(0, blocks, add_block, zeros)

def reference(tokens, assign, state, norm_gain, in_weight, conv_weight, out_weight):
    cache = state
    results = []
    flat_in = in_weight.reshape(D, 3 * D)
    for moment in range(STEPS):
        inputs = tokens[moment].astype(jnp.float32)
        meansq = lax.optimization_barrier(jnp.mean(inputs * inputs, axis=-1, keepdims=True))
        normed = (inputs * lax.rsqrt(meansq + 1e-05) * norm_gain).astype(jnp.bfloat16)
        fresh = block_sum(normed, flat_in, N_NARROW).astype(jnp.bfloat16).reshape(ROWS, 3, D)
        cache = jnp.take(cache, assign[moment].astype(jnp.int32), axis=0)
        mixed = conv_weight[0] * cache[:, 0] + conv_weight[1] * cache[:, 1] + conv_weight[2] * fresh
        cache = jnp.stack([cache[:, 1], fresh], axis=1)
        gated = (mixed[:, 0] * mixed[:, 1] * mixed[:, 2]).astype(jnp.bfloat16)
        results.append(block_sum(gated, out_weight, N_WIDE).astype(jnp.bfloat16))
    return (jnp.stack(results), cache)
```

```python
import jax
import jax.numpy as jnp
from jax import lax
from jax.sharding import PartitionSpec as P

D = 8192


def swap(value, axis, hop):
    count = lax.axis_size(axis)
    return lax.ppermute(value, axis, [(i, i ^ hop) for i in range(count)])


def shards(tokens, assign, state, norm_gain, in_weight, conv_weight, out_weight):
    narrow = lax.axis_size("narrow")
    wide = lax.axis_size("wide")
    steps, rows, feats = tokens.shape
    share = state.shape[0]
    total = narrow * share
    chans = in_weight.shape[2]
    mine = lax.axis_index("narrow")
    direct = wide <= 4
    place = lax.axis_index("wide") if direct else 0
    evens = [2 * k for k in range(narrow // 2)]
    rels = evens + [k + 1 for k in evens]
    half = (narrow // 2) * steps * share
    unit = steps * share

    past = state.transpose(0, 2, 1, 3)
    near = jnp.stack([past] + [swap(past, "narrow", k) for k in evens[1:]])
    far = swap(near, "narrow", 1)
    pool = jnp.concatenate([near, far]).reshape(total, -1)

    if direct:
        blocks = jnp.stack([tokens] + [swap(tokens, "wide", k) for k in range(1, wide)])
    else:
        blocks = lax.all_gather(tokens, "wide", axis=0)
    blocks = blocks.reshape(wide * steps * rows, feats)

    owners = jnp.array(rels, jnp.int32) ^ mine
    slots = (owners[:, None] * share + jnp.arange(share)[None, :])
    first = assign[1][slots]
    wanted = jnp.stack([first, slots], axis=1)
    stage = jnp.arange(steps, dtype=jnp.int32)[None, :, None]
    spot = (((wanted // rows) ^ place) * steps + stage) * rows + wanted % rows
    spot = spot.reshape(-1)
    picker = (spot[:, None] == jnp.arange(wide * steps * rows)[None, :]).astype(jnp.bfloat16)
    ordered = jnp.dot(picker, blocks, preferred_element_type=jnp.float32)
    squares = jnp.sum(ordered * ordered, axis=-1)
    scaled = (ordered * norm_gain).astype(jnp.bfloat16)

    def scatter(partial, kind):
        partial = partial[:half] + swap(partial[half:].astype(kind), "narrow", 1).astype(
            jnp.float32
        )
        result = partial[:unit]
        for index, k in enumerate(evens[1:], 1):
            piece = partial[index * unit : (index + 1) * unit].astype(kind)
            result = result + swap(piece, "narrow", k).astype(jnp.float32)
        return result

    meansq = scatter(squares, jnp.float32) / D
    scale = lax.rsqrt(meansq + 1e-05)[:, None]

    comp = assign[0][lax.dynamic_slice_in_dim(assign[1], mine * share, share, 0)]
    ranks = [rels.index(k) for k in range(narrow)]
    source = jnp.array(ranks, jnp.int32)[(comp // share) ^ mine] * share + comp % share
    chooser = (source[:, None] == jnp.arange(total)[None, :]).astype(jnp.bfloat16)
    kept = jnp.dot(chooser, pool, preferred_element_type=jnp.float32).reshape(share, 3, 2, chans)

    weights = in_weight.transpose(1, 0, 2)
    gates = []
    fresh = []
    for j in range(3):
        product = jnp.dot(scaled, weights[j], preferred_element_type=jnp.float32)
        new = (scatter(product, jnp.bfloat16) * scale).astype(jnp.bfloat16)
        new0, new1 = new[:share], new[share:]
        fresh.append(jnp.stack([new0, new1], axis=1))
        taps = conv_weight[:, j]
        new0, new1 = new0.astype(jnp.float32), new1.astype(jnp.float32)
        mixed0 = taps[0] * kept[:, j, 0] + taps[1] * kept[:, j, 1] + taps[2] * new0
        mixed1 = taps[0] * kept[:, j, 1] + taps[1] * new0 + taps[2] * new1
        gates.append(jnp.concatenate([mixed0, mixed1]))
    memory = jnp.stack(fresh, axis=1).transpose(0, 2, 1, 3)
    gated = (gates[0] * gates[1] * gates[2]).astype(jnp.bfloat16)

    near = jnp.stack([gated] + [swap(gated, "narrow", k) for k in evens[1:]])
    every = jnp.concatenate([near, swap(near, "narrow", 1)]).reshape(narrow * unit, chans)

    order = wanted.reshape(len(rels), steps, share)
    goal = (((order // rows) ^ place) * steps + stage) * rows + order % rows
    goal = goal.reshape(-1)
    sorter = (jnp.arange(wide * steps * rows)[:, None] == goal[None, :]).astype(jnp.bfloat16)
    lined = jnp.dot(sorter, every, preferred_element_type=jnp.float32).astype(jnp.bfloat16)
    partial_out = jnp.dot(lined, out_weight, preferred_element_type=jnp.float32)
    if direct:
        block = steps * rows
        out = partial_out[:block]
        for k in range(1, wide):
            piece = partial_out[k * block : (k + 1) * block].astype(jnp.bfloat16)
            out = out + swap(piece, "wide", k).astype(jnp.float32)
        out = out.astype(jnp.bfloat16)
    else:
        out = lax.psum_scatter(
            partial_out.astype(jnp.bfloat16), "wide", scatter_dimension=0, tiled=True
        )
    return (out.reshape(steps, rows, -1), memory)


def solution(mesh):
    in_specs = (
        P(None, ("groups", "wide"), "narrow"),
        P(None, "groups"),
        P(("groups", "narrow"), None, None, "wide"),
        P("narrow"),
        P("narrow", None, "wide"),
        P(None, None, "wide"),
        P("wide", "narrow"),
    )
    out_specs = (P(None, ("groups", "wide"), "narrow"), P(("groups", "narrow"), None, None, "wide"))
    return jax.shard_map(shards, mesh=mesh, in_specs=in_specs, out_specs=out_specs, check_vma=False)
```

```python
import functools

import jax
import jax.numpy as jnp
from jax import lax
from jax.experimental import pallas as pl
from jax.experimental.pallas import tpu as pltpu
from jax.sharding import PartitionSpec as P

D = 8192
F32 = jnp.float32
BF16 = jnp.bfloat16
LANES = 128


def swap(value, axis, hop):
    count = lax.axis_size(axis)
    return lax.ppermute(value, axis, [(i, i ^ hop) for i in range(count)])


def call(body, outs, args, flops=0, scalars=0):
    whole = pl.BlockSpec(memory_space=pltpu.VMEM)
    small = pl.BlockSpec(memory_space=pltpu.SMEM)
    size = sum(a.size * a.dtype.itemsize for a in (*args, *outs))
    return pl.pallas_call(
        body,
        out_shape=outs,
        in_specs=[small] * scalars + [whole] * (len(args) - scalars),
        out_specs=[whole] * len(outs),
        compiler_params=pltpu.CompilerParams(vmem_limit_bytes=12 << 20),
        cost_estimate=pl.CostEstimate(flops=flops, bytes_accessed=size, transcendentals=0),
    )(*args)


def struct(*shape, dtype=BF16):
    return jax.ShapeDtypeStruct(shape, dtype)


def tiles(width):
    step = min(width, 512)
    return [slice(at, at + step) for at in range(0, width, step)]


def iota(shape, dim):
    return lax.broadcasted_iota(jnp.int32, shape, dim)


def look(keys, table):
    hit = keys == iota((keys.shape[0], table.shape[1]), 1)
    return jnp.sum(jnp.where(hit, table.astype(F32), 0.0), axis=1, keepdims=True).astype(jnp.int32)


def index_body(n, share, steps, rows, ids, assign, picker, chooser):
    mine, place = ids[0], ids[1]
    total = n * share
    unit = steps * share
    row = iota((n * unit, 1), 0)
    rank = lax.div(row, unit)
    rel = jnp.where(rank < n // 2, 2 * rank, 2 * (rank - n // 2) + 1)
    stage = lax.rem(lax.div(row, share), steps)
    slot = (rel ^ mine) * share + lax.rem(row, share)
    wanted = jnp.where(stage == 0, look(slot, assign[1:2, :]), slot)
    spot = ((lax.div(wanted, rows) ^ place) * steps + stage) * rows + lax.rem(wanted, rows)
    hit = spot == iota((n * unit, n * unit), 1)
    picker[...] = jnp.where(hit, 1.0, 0.0).astype(BF16)
    own = iota((share, 1), 0) + mine * share
    cand = look(look(own, assign[1:2, :]), assign[0:1, :])
    rel = lax.div(cand, share) ^ mine
    rank = lax.div(rel, 2) + lax.rem(rel, 2) * (n // 2)
    hit = rank * share + lax.rem(cand, share) == iota((share, total), 1)
    chooser[...] = jnp.where(hit, 1.0, 0.0).astype(BF16)


def split3(value):
    high = value.astype(BF16).astype(F32)
    mid = (value - high).astype(BF16).astype(F32)
    low = value - high - mid
    lane = iota((value.shape[0], LANES), 1)
    return jnp.where(
        lane == 0, high, jnp.where(lane == 1, mid, jnp.where(lane == 2, low, 0.0))
    ).astype(BF16)


def join3(value):
    return jnp.sum(value.astype(F32), axis=1, keepdims=True)


def project_tile(x, weight, keep, send, half):
    for cols in tiles(weight.shape[1]):
        product = jnp.dot(x, weight[:, cols], preferred_element_type=F32)
        keep[:, cols] = product[:half]
        send[:, cols] = product[half:].astype(BF16)


def load_body(weight, *refs):
    outs, sems = refs[:-1], refs[-1]
    copies = [
        pltpu.make_async_copy(weight.at[j], out, sems.at[j]) for j, out in enumerate(outs)
    ]
    for copy in copies:
        copy.start()
    for copy in copies:
        copy.wait()


def load(weight):
    one = struct(*weight.shape[1:])
    size = 2 * weight.size * weight.dtype.itemsize
    return pl.pallas_call(
        load_body,
        out_shape=[one] * 3,
        in_specs=[pl.BlockSpec(memory_space=pltpu.HBM)],
        out_specs=[pl.BlockSpec(memory_space=pltpu.VMEM)] * 3,
        scratch_shapes=[pltpu.SemaphoreType.DMA((3,))],
        compiler_params=pltpu.CompilerParams(vmem_limit_bytes=12 << 20),
        cost_estimate=pl.CostEstimate(flops=0, bytes_accessed=size, transcendentals=0),
    )(weight)


def first_body(half, count, picker, gain, weight, *refs):
    blocks, (scaled, keep, send, squares) = refs[:count], refs[count:]
    x = jnp.concatenate([block[...] for block in blocks]) if count > 1 else blocks[0][...]
    total = jnp.zeros((x.shape[0], 1), F32)
    for cols in tiles(x.shape[1]):
        ordered = jnp.dot(picker[...], x[:, cols], preferred_element_type=F32)
        total = total + jnp.sum(ordered * ordered, axis=1, keepdims=True)
        scaled[:, cols] = (ordered * gain[:, cols]).astype(BF16)
    width = weight.shape[1]
    project_tile(scaled[...], weight, keep, send, half)
    squares[...] = jnp.broadcast_to(total[:half], squares.shape)
    send[:, width:] = split3(total[half:])


def next_body(half, scaled, weight, keep, send):
    project_tile(scaled[...], weight, keep, send, half)


def add_body(unit, with_squares, *refs):
    if with_squares:
        keep, got, squares, own, send, own_squares = refs
    else:
        keep, got, own, send = refs
    width = keep.shape[1]
    for cols in tiles(width):
        own[:, cols] = keep[:unit, cols] + got[:unit, cols].astype(F32)
        send[:, cols] = (keep[unit:, cols] + got[unit:, cols].astype(F32)).astype(BF16)
    if with_squares:
        total = squares[:, :1] + join3(got[:, width:])
        own_squares[...] = jnp.broadcast_to(total[:unit], own_squares.shape)
        send[:, width:] = split3(total[unit:])


def past_body(chooser, conv, near, far, older, newer):
    share = older.shape[1]
    blocks = near.shape[0]
    for j in range(3):
        for cols in tiles(older.shape[2]):
            sums = []
            for k in range(2):
                pool = jnp.concatenate(
                    [near[b, j, k, :, cols] for b in range(blocks)]
                    + [far[b, j, k, :, cols] for b in range(blocks)]
                )
                sums.append(jnp.dot(chooser[...], pool, preferred_element_type=F32))
            first = conv[0, j : j + 1, cols]
            older[j, :, cols] = first * sums[0] + conv[1, j : j + 1, cols] * sums[1]
            newer[j, :, cols] = first * sums[1]


def mix_body(share, peers, conv, older, newer, squares, *refs):
    owns, gots = refs[:3], refs[3 : 3 + 3 * peers]
    gated, fresh = refs[3 + 3 * peers :]
    width = gated.shape[1]
    total = squares[:, :1]
    for p in range(peers):
        total = total + join3(gots[p][:, width:])
    scale = lax.rsqrt(total / D + 1e-05)
    for cols in tiles(width):
        gate = None
        for j in range(3):
            new = owns[j][:, cols]
            for p in range(peers):
                new = new + gots[j * peers + p][:, cols].astype(F32)
            new = (new * scale).astype(BF16)
            new0, new1 = new[:share], new[share:]
            fresh[j, 0, :, cols] = new0
            fresh[j, 1, :, cols] = new1
            new0, new1 = new0.astype(F32), new1.astype(F32)
            last = conv[2, j : j + 1, cols]
            mixed0 = older[j, :, cols] + last * new0
            mixed1 = newer[j, :, cols] + conv[1, j : j + 1, cols] * new0 + last * new1
            mixed = jnp.concatenate([mixed0, mixed1])
            gate = mixed if gate is None else gate * mixed
        gated[:, cols] = gate.astype(BF16)


def out_body(block, picker, near, far, weight, own, *rest):
    rows = near.shape[0] * near.shape[1]
    every = jnp.concatenate(
        [near[b] for b in range(near.shape[0])] + [far[b] for b in range(far.shape[0])]
    )
    lined = lax.dot_general(
        picker[...], every, (((0,), (0,)), ((), ())), preferred_element_type=F32
    ).astype(BF16)
    for cols in tiles(weight.shape[1]):
        product = jnp.dot(lined, weight[:, cols], preferred_element_type=F32)
        own[:, cols] = product[:block].astype(own.dtype)
        for k, ref in enumerate(rest, 1):
            ref[:, cols] = product[k * block : (k + 1) * block].astype(BF16)


def shards(tokens, assign, state, norm_gain, in_weight, conv_weight, out_weight):
    n = lax.axis_size("narrow")
    wide = lax.axis_size("wide")
    steps, rows, feats = tokens.shape
    share = state.shape[0]
    chans = in_weight.shape[2]
    outs = out_weight.shape[1]
    direct = wide <= 4
    mine = lax.axis_index("narrow")
    place = lax.axis_index("wide") if direct else 0
    evens = [2 * k for k in range(n // 2)]
    unit = steps * share
    half = (n // 2) * unit
    peers = n // 2 - 1
    block = steps * rows

    mine_tokens = tokens.reshape(block, feats)
    if direct:
        blocks = [mine_tokens] + [swap(mine_tokens, "wide", k) for k in range(1, wide)]
    else:
        blocks = [lax.all_gather(mine_tokens, "wide", axis=0, tiled=True)]

    past = state.transpose(2, 1, 0, 3)
    near = jnp.stack([past] + [swap(past, "narrow", k) for k in evens[1:]])
    far = swap(near, "narrow", 1)

    ids = jnp.stack([mine, place]).astype(jnp.int32)
    picker, chooser = call(
        functools.partial(index_body, n, share, steps, rows),
        [struct(n * unit, n * unit), struct(share, n * share)],
        [ids, assign],
        scalars=1,
    )
    weights = load(in_weight.transpose(1, 0, 2))
    cost = 2 * n * unit * feats * chans
    keeps, sends = [None] * 3, [None] * 3
    scaled, keeps[0], sends[0], squares = call(
        functools.partial(first_body, half, len(blocks)),
        [
            struct(n * unit, feats),
            struct(half, chans, dtype=F32),
            struct(half, chans + LANES),
            struct(half, LANES, dtype=F32),
        ],
        [picker, norm_gain.reshape(1, feats), weights[0], *blocks],
        flops=cost,
    )
    for j in (1, 2):
        keeps[j], sends[j] = call(
            functools.partial(next_body, half),
            [struct(half, chans, dtype=F32), struct(half, chans)],
            [scaled, weights[j]],
            flops=cost,
        )
    owns, gots = [None] * 3, []
    for j in range(3):
        got = swap(sends[j], "narrow", 1)
        extra = LANES if j == 0 else 0
        shapes = [struct(unit, chans, dtype=F32), struct(half - unit, chans + extra)]
        args = [keeps[j], got]
        if j == 0:
            shapes.append(struct(unit, LANES, dtype=F32))
            args.append(squares)
        result = call(functools.partial(add_body, unit, j == 0), shapes, args)
        owns[j] = result[0]
        if j == 0:
            squares = result[2]
        for p, k in enumerate(evens[1:]):
            gots.append(swap(result[1][p * unit : (p + 1) * unit], "narrow", k))
    older, newer = call(
        past_body,
        [struct(3, share, chans, dtype=F32)] * 2,
        [chooser, conv_weight, near, far],
        flops=2 * share * n * share * 6 * chans,
    )
    gated, fresh = call(
        functools.partial(mix_body, share, peers),
        [struct(unit, chans), struct(3, 2, share, chans)],
        [conv_weight, older, newer, squares, *owns, *gots],
    )
    memory = fresh.transpose(2, 1, 0, 3)

    near = jnp.stack([gated] + [swap(gated, "narrow", k) for k in evens[1:]])
    far = swap(near, "narrow", 1)
    cost = 2 * n * unit * chans * outs
    if direct:
        own, *rest = call(
            functools.partial(out_body, block),
            [struct(block, outs, dtype=F32)] + [struct(block, outs)] * (wide - 1),
            [picker, near, far, out_weight],
            flops=cost,
        )
        for k in range(1, wide):
            own = own + swap(rest[k - 1], "wide", k).astype(F32)
        out = own.astype(BF16)
    else:
        (partial,) = call(
            functools.partial(out_body, n * unit),
            [struct(n * unit, outs)],
            [picker, near, far, out_weight],
            flops=cost,
        )
        out = lax.psum_scatter(partial, "wide", scatter_dimension=0, tiled=True)
    return (out.reshape(steps, rows, outs), memory)


def solution(mesh):
    in_specs = (
        P(None, ("groups", "wide"), "narrow"),
        P(None, "groups"),
        P(("groups", "narrow"), None, None, "wide"),
        P("narrow"),
        P("narrow", None, "wide"),
        P(None, None, "wide"),
        P("wide", "narrow"),
    )
    out_specs = (P(None, ("groups", "wide"), "narrow"), P(("groups", "narrow"), None, None, "wide"))
    return jax.shard_map(shards, mesh=mesh, in_specs=in_specs, out_specs=out_specs, check_vma=False)
```

```python
import functools

import jax
import jax.numpy as jnp
from jax import lax
from jax.experimental import pallas as pl
from jax.experimental.pallas import tpu as pltpu
from jax.sharding import PartitionSpec as P

D = 8192
F32 = jnp.float32
BF16 = jnp.bfloat16
LANES = 128
GROUPS = ((0,), (1,), (2,))


def swap(value, axis, hop):
    count = lax.axis_size(axis)
    return lax.ppermute(value, axis, [(i, i ^ hop) for i in range(count)])


def call(body, outs, args, flops=0, scalars=0):
    whole = pl.BlockSpec(memory_space=pltpu.VMEM)
    small = pl.BlockSpec(memory_space=pltpu.SMEM)
    size = sum(a.size * a.dtype.itemsize for a in (*args, *outs))
    return pl.pallas_call(
        body,
        out_shape=outs,
        in_specs=[small] * scalars + [whole] * (len(args) - scalars),
        out_specs=[whole] * len(outs),
        compiler_params=pltpu.CompilerParams(vmem_limit_bytes=12 << 20),
        cost_estimate=pl.CostEstimate(flops=flops, bytes_accessed=size, transcendentals=0),
    )(*args)


def struct(*shape, dtype=BF16):
    return jax.ShapeDtypeStruct(shape, dtype)


def tiles(width):
    step = next(size for size in (512, 256, 128, width) if width % size == 0)
    return [slice(at, at + step) for at in range(0, width, step)]


def iota(shape, dim):
    return lax.broadcasted_iota(jnp.int32, shape, dim)


def look(keys, table):
    hit = keys == iota((keys.shape[0], table.shape[1]), 1)
    return jnp.sum(jnp.where(hit, table.astype(F32), 0.0), axis=1, keepdims=True).astype(jnp.int32)


def index_body(n, share, rows, mine, place, assign, first, second):
    total = n * share
    row = iota((total, 1), 0)
    rank = lax.div(row, share)
    rel = jnp.where(rank < n // 2, 2 * rank, 2 * (rank - n // 2) + 1)
    slot = (rel ^ mine) * share + lax.rem(row, share)
    for picker, wanted in ((first, look(slot, assign[1:2, :])), (second, slot)):
        spot = (lax.div(wanted, rows) ^ place) * rows + lax.rem(wanted, rows)
        hit = spot == iota((total, total), 1)
        picker[...] = jnp.where(hit, 1.0, 0.0).astype(BF16)


def load_body(n, share, rows, direct, assign, weight, first, second, *refs):
    outs, (table, sems) = refs[:-2], refs[-2:]
    fetch = pltpu.make_async_copy(assign, table, sems.at[len(outs)])
    fetch.start()
    copies = [
        pltpu.make_async_copy(weight.at[j], out, sems.at[j]) for j, out in enumerate(outs)
    ]
    for copy in copies:
        copy.start()
    mine = lax.axis_index("narrow")
    place = lax.axis_index("wide") if direct else 0
    fetch.wait()
    index_body(n, share, rows, mine, place, table, first, second)
    for copy in copies:
        copy.wait()


def load(n, share, rows, direct, assign, weight):
    one = struct(*weight.shape[1:])
    size = 2 * weight.size * weight.dtype.itemsize
    vmem = pl.BlockSpec(memory_space=pltpu.VMEM)
    hbm = pl.BlockSpec(memory_space=pltpu.HBM)
    return pl.pallas_call(
        functools.partial(load_body, n, share, rows, direct),
        out_shape=[struct(n * share, n * share)] * 2 + [one] * 3,
        in_specs=[hbm, hbm],
        out_specs=[vmem] * 5,
        scratch_shapes=[pltpu.VMEM(assign.shape, jnp.int32), pltpu.SemaphoreType.DMA((4,))],
        compiler_params=pltpu.CompilerParams(vmem_limit_bytes=12 << 20),
        cost_estimate=pl.CostEstimate(flops=0, bytes_accessed=size, transcendentals=0),
    )(assign, weight)


def split3(value):
    high = value.astype(BF16).astype(F32)
    mid = (value - high).astype(BF16).astype(F32)
    low = value - high - mid
    lane = iota((value.shape[0], LANES), 1)
    return jnp.where(
        lane == 0, high, jnp.where(lane == 1, mid, jnp.where(lane == 2, low, 0.0))
    ).astype(BF16)


def join3(value):
    return jnp.sum(value.astype(F32), axis=1, keepdims=True)


def project_tiles(scaled, weights, keep, send):
    half = keep.shape[0]
    for j, weight in enumerate(weights):
        width = weight.shape[1]
        for cols in tiles(width):
            product = jnp.dot(scaled[...], weight[:, cols], preferred_element_type=F32)
            at = slice(j * width + cols.start, j * width + cols.stop)
            keep[:, at] = product[:half]
            send[:, at] = product[half:].astype(BF16)


def first_body(share, rows, steps, order, first, second, gain, *refs):
    count = 1 + len(order)
    blocks, weights = refs[:count], refs[count:-4]
    blocks = [blocks[0]] + [blocks[1 + order.index(k)] for k in range(1, count)]
    scaled, keep, send, squares = refs[-4:]
    length, feats = blocks[0].shape
    total = first.shape[0]
    half, width = keep.shape
    for stage, picker in enumerate((first, second)):
        x = jnp.concatenate(
            [
                block[at : at + rows, :]
                for block in blocks
                for at in range(stage * rows, length, steps * rows)
            ]
        )
        sums = jnp.zeros((total, 1), F32)
        spots = [
            (slice(at, at + share), slice(at * steps + stage * share, at * steps + (stage + 1) * share))
            for at in range(0, total, share)
        ]
        for cols in tiles(feats):
            ordered = jnp.dot(picker[...], x[:, cols], preferred_element_type=F32)
            sums = sums + jnp.sum(ordered * ordered, axis=1, keepdims=True)
            value = (ordered * gain[:, cols]).astype(BF16)
            for source, target in spots:
                scaled[target, cols] = value[source]
        for source, target in spots:
            if target.start < half:
                squares[target, :] = jnp.broadcast_to(sums[source], (share, LANES))
            else:
                send[target.start - half : target.stop - half, width:] = split3(sums[source])
    project_tiles(scaled, weights, keep, send)


def next_body(scaled, *refs):
    *weights, keep, send = refs
    project_tiles(scaled, weights, keep, send)


def add_body(unit, with_squares, keep, got, *refs):
    width = keep.shape[1]
    if with_squares:
        squares, own, own_squares, *sends = refs
        total = squares[:, :1] + join3(got[:, width:])
        own_squares[...] = jnp.broadcast_to(total[:unit], own_squares.shape)
    else:
        own, *sends = refs
    for cols in tiles(width):
        own[:, cols] = keep[:unit, cols] + got[:unit, cols].astype(F32)
        for p, send in enumerate(sends, 1):
            part = slice(p * unit, (p + 1) * unit)
            send[:, cols] = (keep[part, cols] + got[part, cols].astype(F32)).astype(BF16)
    if with_squares:
        for p, send in enumerate(sends, 1):
            send[:, width:] = split3(total[p * unit : (p + 1) * unit])


def past_body(n, share, assign, conv, *refs):
    pools, (older, newer) = refs[:n], refs[n:]
    mine = lax.axis_index("narrow")

    def one(row, carry):
        cand = assign[0, assign[1, mine * share + row]]
        rel = lax.div(cand, share) ^ mine
        spot = lax.rem(cand, share)
        for j in range(3):
            both = pools[0][spot, j].astype(F32)
            for k in range(1, n):
                both = jnp.where(rel == k, pools[k][spot, j].astype(F32), both)
            first = conv[0, j : j + 1, :]
            older[j, pl.ds(row, 1), :] = first * both[0:1] + conv[1, j : j + 1, :] * both[1:2]
            newer[j, pl.ds(row, 1), :] = first * both[1:2]
        return carry

    lax.fori_loop(0, share, one, 0)


def mix_body(share, peers, groups, conv, older, newer, squares, *refs):
    gated, fresh = refs[-2:]
    owns = refs[: len(groups)]
    gots = [refs[at : at + peers] for at in range(len(groups), len(refs) - 2, peers)]
    width = gated.shape[1]
    total = squares[:, :1]
    for got in gots[0]:
        total = total + join3(got[:, owns[0].shape[1] :])
    scale = lax.rsqrt(total / D + 1e-05)
    for cols in tiles(width):
        gate = None
        for g, group in enumerate(groups):
            for at, j in enumerate(group):
                spot = slice(at * width + cols.start, at * width + cols.stop)
                new = owns[g][:, spot]
                for got in gots[g]:
                    new = new + got[:, spot].astype(F32)
                new = (new * scale).astype(BF16)
                new0, new1 = new[:share], new[share:]
                fresh[j, 0, :, cols] = new0
                fresh[j, 1, :, cols] = new1
                new0, new1 = new0.astype(F32), new1.astype(F32)
                last = conv[2, j : j + 1, cols]
                mixed0 = older[j, :, cols] + last * new0
                mixed1 = newer[j, :, cols] + conv[1, j : j + 1, cols] * new0 + last * new1
                mixed = jnp.concatenate([mixed0, mixed1])
                gate = mixed if gate is None else gate * mixed
        gated[:, cols] = gate.astype(BF16)


def out_body(n, share, rows, first, second, weight, *refs):
    pieces, own, rest = refs[:n], refs[n], refs[n + 1 :]
    lined = []
    for stage, picker in enumerate((first, second)):
        part = slice(stage * share, (stage + 1) * share)
        every = jnp.concatenate([piece[part, :] for piece in pieces])
        lined.append(
            lax.dot_general(
                picker[...], every, (((0,), (0,)), ((), ())), preferred_element_type=F32
            ).astype(BF16)
        )
    blocks = range(0, first.shape[0], rows)
    lined = jnp.concatenate([part[at : at + rows] for at in blocks for part in lined])
    block = own.shape[0]
    for cols in tiles(weight.shape[1]):
        product = jnp.dot(lined, weight[:, cols], preferred_element_type=F32)
        own[:, cols] = product[:block].astype(own.dtype)
        for k, ref in enumerate(rest, 1):
            ref[:, cols] = product[k * block : (k + 1) * block].astype(BF16)


def shards(tokens, assign, state, norm_gain, in_weight, conv_weight, out_weight):
    n = lax.axis_size("narrow")
    wide = lax.axis_size("wide")
    steps, rows, feats = tokens.shape
    share = state.shape[0]
    chans = in_weight.shape[2]
    outs = out_weight.shape[1]
    direct = wide <= 4
    order = [k for k in (2, 3, 1) if k < wide]
    evens = [2 * k for k in range(n // 2)]
    total = n * share
    half = total // 2

    mine_tokens = tokens.reshape(steps * rows, feats)
    if direct:
        blocks = [mine_tokens] + [swap(mine_tokens, "wide", k) for k in order]
    else:
        blocks = [lax.all_gather(mine_tokens, "wide", axis=0, tiled=True)]

    past = state.transpose(0, 2, 1, 3)
    pools = [past] * n
    for k in evens:
        pools[k] = swap(past, "narrow", k) if k else past
        pools[k + 1] = swap(pools[k], "narrow", 1)

    *pickers, w0, w1, w2 = load(n, share, rows, direct, assign, in_weight.transpose(1, 0, 2))
    weights = [w0, w1, w2]
    older, newer = call(
        functools.partial(past_body, n, share),
        [struct(3, share, chans, dtype=F32)] * 2,
        [assign, conv_weight, *pools],
        scalars=1,
    )

    unit = steps * share
    cost = 2 * steps * total * feats * chans
    owns, gots = [], []
    for group in GROUPS:
        first = not owns
        width = chans * len(group)
        wider = width + LANES * first
        shapes = [struct(steps * half, width, dtype=F32), struct(steps * half, wider)]
        if first:
            scaled, keep, send, squares = call(
                functools.partial(first_body, share, rows, steps, order if direct else []),
                [struct(steps * total, feats), *shapes, struct(steps * half, LANES, dtype=F32)],
                [*pickers, norm_gain.reshape(1, feats), *blocks, *(weights[j] for j in group)],
                flops=cost * len(group),
            )
        else:
            keep, send = call(
                next_body,
                shapes,
                [scaled, *(weights[j] for j in group)],
                flops=cost * len(group),
            )
        extra = [squares] if first else []
        kept = [struct(unit, width, dtype=F32)] + [struct(unit, LANES, dtype=F32)] * len(extra)
        result = call(
            functools.partial(add_body, unit, first),
            kept + [struct(unit, wider)] * (n // 2 - 1),
            [keep, swap(send, "narrow", 1), *extra],
        )
        owns.append(result[0])
        if first:
            squares = result[1]
        gots += [swap(p, "narrow", k) for p, k in zip(result[len(kept) :], evens[1:])]
    gated, fresh = call(
        functools.partial(mix_body, share, n // 2 - 1, GROUPS),
        [struct(unit, chans), struct(3, 2, share, chans)],
        [conv_weight, older, newer, squares, *owns, *gots],
    )
    near = [swap(gated, "narrow", k) if k else gated for k in evens]
    far = [swap(piece, "narrow", 1) for piece in near]
    block = steps * rows
    shapes = [struct(steps * total, outs)]
    if direct:
        shapes = [struct(block, outs, dtype=F32)] + [struct(block, outs)] * (wide - 1)
    out, *parts = call(
        functools.partial(out_body, n, share, rows),
        shapes,
        [*pickers, out_weight, *near, *far],
        flops=2 * steps * total * chans * outs,
    )
    if direct:
        for k in order:
            out = out + swap(parts[k - 1], "wide", k).astype(F32)
        out = out.astype(BF16)
    else:
        out = lax.psum_scatter(out, "wide", scatter_dimension=0, tiled=True)
    return (out.reshape(steps, rows, outs), fresh.transpose(2, 1, 0, 3))


def solution(mesh):
    in_specs = (
        P(None, ("groups", "wide"), "narrow"),
        P(None, "groups"),
        P(("groups", "narrow"), None, None, "wide"),
        P("narrow"),
        P("narrow", None, "wide"),
        P(None, None, "wide"),
        P("wide", "narrow"),
    )
    out_specs = (P(None, ("groups", "wide"), "narrow"), P(("groups", "narrow"), None, None, "wide"))
    return jax.shard_map(shards, mesh=mesh, in_specs=in_specs, out_specs=out_specs, check_vma=False)
```

```python
import functools

import jax
import jax.numpy as jnp
from jax import lax
from jax.experimental import pallas as pl
from jax.experimental.pallas import tpu as pltpu
from jax.sharding import PartitionSpec as P

D = 8192
F32 = jnp.float32
BF16 = jnp.bfloat16
LANES = 128
GROUPS = ((0,), (1,), (2,))


def swap(value, axis, hop):
    count = lax.axis_size(axis)
    return lax.ppermute(value, axis, [(i, i ^ hop) for i in range(count)])


def call(body, outs, args, flops=0, scalars=0):
    whole = pl.BlockSpec(memory_space=pltpu.VMEM)
    small = pl.BlockSpec(memory_space=pltpu.SMEM)
    size = sum(a.size * a.dtype.itemsize for a in (*args, *outs))
    return pl.pallas_call(
        body,
        out_shape=outs,
        in_specs=[small] * scalars + [whole] * (len(args) - scalars),
        out_specs=[whole] * len(outs),
        compiler_params=pltpu.CompilerParams(vmem_limit_bytes=12 << 20),
        cost_estimate=pl.CostEstimate(flops=flops, bytes_accessed=size, transcendentals=0),
    )(*args)


def struct(*shape, dtype=BF16):
    return jax.ShapeDtypeStruct(shape, dtype)


def tiles(width):
    step = next(size for size in (512, 256, 128, width) if width % size == 0)
    return [slice(at, at + step) for at in range(0, width, step)]


def iota(shape, dim):
    return lax.broadcasted_iota(jnp.int32, shape, dim)


def look(keys, table):
    hit = keys == iota((keys.shape[0], table.shape[1]), 1)
    return jnp.sum(jnp.where(hit, table.astype(F32), 0.0), axis=1, keepdims=True).astype(jnp.int32)


def index_body(n, share, rows, mine, place, assign, first, second):
    total = n * share
    row = iota((total, 1), 0)
    rank = lax.div(row, share)
    rel = jnp.where(rank < n // 2, 2 * rank, 2 * (rank - n // 2) + 1)
    slot = (rel ^ mine) * share + lax.rem(row, share)
    for picker, wanted in ((first, look(slot, assign[1:2, :])), (second, slot)):
        spot = (lax.div(wanted, rows) ^ place) * rows + lax.rem(wanted, rows)
        hit = spot == iota((total, total), 1)
        picker[...] = jnp.where(hit, 1.0, 0.0).astype(BF16)


def load_body(n, share, rows, direct, assign, weight, first, second, *refs):
    outs, (table, sems) = refs[:-2], refs[-2:]
    fetch = pltpu.make_async_copy(assign, table, sems.at[len(outs)])
    fetch.start()
    copies = [
        pltpu.make_async_copy(weight.at[j], out, sems.at[j]) for j, out in enumerate(outs)
    ]
    for copy in copies:
        copy.start()
    mine = lax.axis_index("narrow")
    place = lax.axis_index("wide") if direct else 0
    fetch.wait()
    index_body(n, share, rows, mine, place, table, first, second)
    for copy in copies:
        copy.wait()


def load(n, share, rows, direct, assign, weight):
    one = struct(*weight.shape[1:])
    size = 2 * weight.size * weight.dtype.itemsize
    vmem = pl.BlockSpec(memory_space=pltpu.VMEM)
    hbm = pl.BlockSpec(memory_space=pltpu.HBM)
    return pl.pallas_call(
        functools.partial(load_body, n, share, rows, direct),
        out_shape=[struct(n * share, n * share)] * 2 + [one] * 3,
        in_specs=[hbm, hbm],
        out_specs=[vmem] * 5,
        scratch_shapes=[pltpu.VMEM(assign.shape, jnp.int32), pltpu.SemaphoreType.DMA((4,))],
        compiler_params=pltpu.CompilerParams(vmem_limit_bytes=12 << 20),
        cost_estimate=pl.CostEstimate(flops=0, bytes_accessed=size, transcendentals=0),
    )(assign, weight)


def split3(value):
    high = value.astype(BF16).astype(F32)
    mid = (value - high).astype(BF16).astype(F32)
    low = value - high - mid
    lane = iota((value.shape[0], LANES), 1)
    return jnp.where(
        lane == 0, high, jnp.where(lane == 1, mid, jnp.where(lane == 2, low, 0.0))
    ).astype(BF16)


def join3(value):
    return jnp.sum(value.astype(F32), axis=1, keepdims=True)


def project_tiles(scaled, weights, keep, send):
    half = keep.shape[0]
    for j, weight in enumerate(weights):
        width = weight.shape[1]
        for cols in tiles(width):
            product = jnp.dot(scaled[...], weight[:, cols], preferred_element_type=F32)
            at = slice(j * width + cols.start, j * width + cols.stop)
            keep[:, at] = product[:half]
            send[:, at] = product[half:].astype(BF16)


def first_body(share, rows, steps, order, first, second, gain, *refs):
    count = 1 + len(order)
    blocks, weights = refs[:count], refs[count:-4]
    blocks = [blocks[0]] + [blocks[1 + order.index(k)] for k in range(1, count)]
    scaled, keep, send, squares = refs[-4:]
    length, feats = blocks[0].shape
    total = first.shape[0]
    half, width = keep.shape
    for stage, picker in enumerate((first, second)):
        x = jnp.concatenate(
            [
                block[at : at + rows, :]
                for block in blocks
                for at in range(stage * rows, length, steps * rows)
            ]
        )
        sums = jnp.zeros((total, 1), F32)
        spots = [
            (slice(at, at + share), slice(at * steps + stage * share, at * steps + (stage + 1) * share))
            for at in range(0, total, share)
        ]
        for cols in tiles(feats):
            ordered = jnp.dot(picker[...], x[:, cols], preferred_element_type=F32)
            sums = sums + jnp.sum(ordered * ordered, axis=1, keepdims=True)
            value = (ordered * gain[:, cols]).astype(BF16)
            for source, target in spots:
                scaled[target, cols] = value[source]
        for source, target in spots:
            if target.start < half:
                squares[target, :] = jnp.broadcast_to(sums[source], (share, LANES))
            else:
                send[target.start - half : target.stop - half, width:] = split3(sums[source])
    project_tiles(scaled, weights, keep, send)


def next_body(scaled, *refs):
    *weights, keep, send = refs
    project_tiles(scaled, weights, keep, send)


def add_body(unit, with_squares, cuts, keep, got, *refs):
    width = keep.shape[1]
    if with_squares:
        squares, own, own_squares, *sends = refs
        total = squares[:, :1] + join3(got[:, width:])
        own_squares[...] = jnp.broadcast_to(total[:unit], own_squares.shape)
    else:
        own, *sends = refs
    piece = width // cuts
    for cols in tiles(piece):
        for cut in range(cuts):
            at = slice(cut * piece + cols.start, cut * piece + cols.stop)
            own[:, at] = keep[:unit, at] + got[:unit, at].astype(F32)
            for p, send in enumerate(sends[cut::cuts], 1):
                part = slice(p * unit, (p + 1) * unit)
                send[:, cols] = (keep[part, at] + got[part, at].astype(F32)).astype(BF16)
    if with_squares:
        for p, send in enumerate(sends, 1):
            send[:, width:] = split3(total[p * unit : (p + 1) * unit])


def past_body(n, share, assign, conv, *refs):
    pools, (older, newer) = refs[:n], refs[n:]
    mine = lax.axis_index("narrow")

    def one(row, carry):
        cand = assign[0, assign[1, mine * share + row]]
        rel = lax.div(cand, share) ^ mine
        spot = lax.rem(cand, share)
        for j in range(3):
            both = pools[0][spot, j].astype(F32)
            for k in range(1, n):
                both = jnp.where(rel == k, pools[k][spot, j].astype(F32), both)
            first = conv[0, j : j + 1, :]
            older[j, pl.ds(row, 1), :] = first * both[0:1] + conv[1, j : j + 1, :] * both[1:2]
            newer[j, pl.ds(row, 1), :] = first * both[1:2]
        return carry

    lax.fori_loop(0, share, one, 0)


def mix_body(share, peers, cut, conv, older, newer, squares, *refs):
    owns, gots, (gated, fresh) = refs[:3], refs[3:-2], refs[-2:]
    width = gated.shape[1]
    total = squares[:, :1]
    for got in gots[:peers]:
        total = total + join3(got[:, owns[0].shape[1] :])
    scale = lax.rsqrt(total / D + 1e-05)
    for cols in tiles(width):
        at = slice(cut * width + cols.start, cut * width + cols.stop)
        gate = None
        for j in range(3):
            new = owns[j][:, at]
            for got in gots[j * peers : (j + 1) * peers]:
                new = new + got[:, cols if j == 2 else at].astype(F32)
            new = (new * scale).astype(BF16)
            new0, new1 = new[:share], new[share:]
            fresh[j, 0, :, cols] = new0
            fresh[j, 1, :, cols] = new1
            new0, new1 = new0.astype(F32), new1.astype(F32)
            last = conv[2, j : j + 1, at]
            mixed0 = older[j, :, at] + last * new0
            mixed1 = newer[j, :, at] + conv[1, j : j + 1, at] * new0 + last * new1
            mixed = jnp.concatenate([mixed0, mixed1])
            gate = mixed if gate is None else gate * mixed
        gated[:, cols] = gate.astype(BF16)


def out_body(n, cuts, share, rows, first, second, weight, *refs):
    pieces, own, rest = refs[: n * cuts], refs[n * cuts], refs[n * cuts + 1 :]
    blocks = range(0, first.shape[0], rows)
    lined = []
    for stage, picker in enumerate((first, second)):
        part = slice(stage * share, (stage + 1) * share)
        sides = []
        for cut in range(cuts):
            every = jnp.concatenate([piece[part, :] for piece in pieces[cut * n : (cut + 1) * n]])
            sides.append(
                lax.dot_general(
                    picker[...], every, (((0,), (0,)), ((), ())), preferred_element_type=F32
                ).astype(BF16)
            )
        lined.append(jnp.concatenate(sides, axis=1))
    lined = jnp.concatenate([part[at : at + rows] for at in blocks for part in lined])
    block = own.shape[0]
    for cols in tiles(weight.shape[1]):
        product = jnp.dot(lined, weight[:, cols], preferred_element_type=F32)
        own[:, cols] = product[:block].astype(own.dtype)
        for k, ref in enumerate(rest, 1):
            ref[:, cols] = product[k * block : (k + 1) * block].astype(BF16)


def shards(tokens, assign, state, norm_gain, in_weight, conv_weight, out_weight):
    n = lax.axis_size("narrow")
    wide = lax.axis_size("wide")
    steps, rows, feats = tokens.shape
    share = state.shape[0]
    chans = in_weight.shape[2]
    outs = out_weight.shape[1]
    direct = wide <= 4
    order = [k for k in (2, 3, 1) if k < wide]
    evens = [2 * k for k in range(n // 2)]
    total = n * share
    half = total // 2

    mine_tokens = tokens.reshape(steps * rows, feats)
    if direct:
        blocks = [mine_tokens] + [swap(mine_tokens, "wide", k) for k in order]
    else:
        blocks = [lax.all_gather(mine_tokens, "wide", axis=0, tiled=True)]

    past = state.transpose(0, 2, 1, 3)
    pools = [past] * n
    for k in evens:
        pools[k] = swap(past, "narrow", k) if k else past
        pools[k + 1] = swap(pools[k], "narrow", 1)

    *pickers, w0, w1, w2 = load(n, share, rows, direct, assign, in_weight.transpose(1, 0, 2))
    weights = [w0, w1, w2]
    older, newer = call(
        functools.partial(past_body, n, share),
        [struct(3, share, chans, dtype=F32)] * 2,
        [assign, conv_weight, *pools],
        scalars=1,
    )

    unit = steps * share
    cost = 2 * steps * total * feats * chans
    owns, gots = [], []
    for group in GROUPS:
        first = not owns
        width = chans * len(group)
        wider = width + LANES * first
        shapes = [struct(steps * half, width, dtype=F32), struct(steps * half, wider)]
        if first:
            scaled, keep, send, squares = call(
                functools.partial(first_body, share, rows, steps, order if direct else []),
                [struct(steps * total, feats), *shapes, struct(steps * half, LANES, dtype=F32)],
                [*pickers, norm_gain.reshape(1, feats), *blocks, *(weights[j] for j in group)],
                flops=cost * len(group),
            )
        else:
            keep, send = call(
                next_body,
                shapes,
                [scaled, *(weights[j] for j in group)],
                flops=cost * len(group),
            )
        cuts = 2 if len(owns) == 2 and chans % (2 * LANES) == 0 else 1
        extra = [squares] if first else []
        kept = [struct(unit, width, dtype=F32)] + [struct(unit, LANES, dtype=F32)] * len(extra)
        result = call(
            functools.partial(add_body, unit, first, cuts),
            kept + [struct(unit, wider // cuts)] * ((n // 2 - 1) * cuts),
            [keep, swap(send, "narrow", 1), *extra],
        )
        owns.append(result[0])
        if first:
            squares = result[1]
        leaving = result[len(kept) :]
        gots += [
            [swap(p, "narrow", k) for p, k in zip(leaving[cut::cuts], evens[1:])]
            for cut in range(cuts)
        ]
    fresh, near, far = [], [], []
    for cut in range(cuts):
        gated, part = call(
            functools.partial(mix_body, share, n // 2 - 1, cut),
            [struct(unit, chans // cuts), struct(3, 2, share, chans // cuts)],
            [conv_weight, older, newer, squares, *owns, *gots[0], *gots[1], *gots[2 + cut]],
        )
        fresh.append(part)
        near.append([swap(gated, "narrow", k) if k else gated for k in evens])
        far.append([swap(piece, "narrow", 1) for piece in near[-1]])
    fresh = jnp.concatenate(fresh, axis=3)
    pieces = [piece for cut in range(cuts) for piece in near[cut] + far[cut]]
    block = steps * rows
    shapes = [struct(steps * total, outs)]
    if direct:
        shapes = [struct(block, outs, dtype=F32)] + [struct(block, outs)] * (wide - 1)
    out, *parts = call(
        functools.partial(out_body, n, cuts, share, rows),
        shapes,
        [*pickers, out_weight, *pieces],
        flops=2 * steps * total * chans * outs,
    )
    if direct:
        for k in [k for k in (2, 1, 3) if k < wide]:
            out = out + swap(parts[k - 1], "wide", k).astype(F32)
        out = out.astype(BF16)
    else:
        out = lax.psum_scatter(out, "wide", scatter_dimension=0, tiled=True)
    return (out.reshape(steps, rows, outs), fresh.transpose(2, 1, 0, 3))


def solution(mesh):
    in_specs = (
        P(None, ("groups", "wide"), "narrow"),
        P(None, "groups"),
        P(("groups", "narrow"), None, None, "wide"),
        P("narrow"),
        P("narrow", None, "wide"),
        P(None, None, "wide"),
        P("wide", "narrow"),
    )
    out_specs = (P(None, ("groups", "wide"), "narrow"), P(("groups", "narrow"), None, None, "wide"))
    return jax.shard_map(shards, mesh=mesh, in_specs=in_specs, out_specs=out_specs, check_vma=False)
```

```python
import functools

import jax
import jax.numpy as jnp
from jax import lax
from jax.experimental import pallas as pl
from jax.experimental.pallas import tpu as pltpu
from jax.sharding import PartitionSpec as P

D = 8192
F32 = jnp.float32
BF16 = jnp.bfloat16
LANES = 128
GROUPS = ((0,), (1,), (2,))


def swap(value, axis, hop):
    count = lax.axis_size(axis)
    return lax.ppermute(value, axis, [(i, i ^ hop) for i in range(count)])


def call(body, outs, args, flops=0, scalars=0):
    whole = pl.BlockSpec(memory_space=pltpu.VMEM)
    small = pl.BlockSpec(memory_space=pltpu.SMEM)
    size = sum(a.size * a.dtype.itemsize for a in (*args, *outs))
    return pl.pallas_call(
        body,
        out_shape=outs,
        in_specs=[small] * scalars + [whole] * (len(args) - scalars),
        out_specs=[whole] * len(outs),
        compiler_params=pltpu.CompilerParams(vmem_limit_bytes=12 << 20),
        cost_estimate=pl.CostEstimate(flops=flops, bytes_accessed=size, transcendentals=0),
    )(*args)


def struct(*shape, dtype=BF16):
    return jax.ShapeDtypeStruct(shape, dtype)


def tiles(width):
    step = next(size for size in (512, 256, 128, width) if width % size == 0)
    return [slice(at, at + step) for at in range(0, width, step)]


def iota(shape, dim):
    return lax.broadcasted_iota(jnp.int32, shape, dim)


def look(keys, table):
    hit = keys == iota((keys.shape[0], table.shape[1]), 1)
    return jnp.sum(jnp.where(hit, table.astype(F32), 0.0), axis=1, keepdims=True).astype(jnp.int32)


def index_body(n, share, rows, mine, place, assign, first, second):
    total = n * share
    row = iota((total, 1), 0)
    rank = lax.div(row, share)
    rel = jnp.where(rank < n // 2, 2 * rank, 2 * (rank - n // 2) + 1)
    slot = (rel ^ mine) * share + lax.rem(row, share)
    for picker, wanted in ((first, look(slot, assign[1:2, :])), (second, slot)):
        spot = (lax.div(wanted, rows) ^ place) * rows + lax.rem(wanted, rows)
        hit = spot == iota((total, total), 1)
        picker[...] = jnp.where(hit, 1.0, 0.0).astype(BF16)


def load_body(n, share, rows, direct, assign, weight, first, second, *refs):
    outs, (table, sems) = refs[:-2], refs[-2:]
    fetch = pltpu.make_async_copy(assign, table, sems.at[len(outs)])
    fetch.start()
    copies = [
        pltpu.make_async_copy(weight.at[j], out, sems.at[j]) for j, out in enumerate(outs)
    ]
    for copy in copies:
        copy.start()
    mine = lax.axis_index("narrow")
    place = lax.axis_index("wide") if direct else 0
    fetch.wait()
    index_body(n, share, rows, mine, place, table, first, second)
    for copy in copies:
        copy.wait()


def load(n, share, rows, direct, assign, weight):
    one = struct(*weight.shape[1:])
    size = 2 * weight.size * weight.dtype.itemsize
    vmem = pl.BlockSpec(memory_space=pltpu.VMEM)
    hbm = pl.BlockSpec(memory_space=pltpu.HBM)
    return pl.pallas_call(
        functools.partial(load_body, n, share, rows, direct),
        out_shape=[struct(n * share, n * share)] * 2 + [one] * 3,
        in_specs=[hbm, hbm],
        out_specs=[vmem] * 5,
        scratch_shapes=[pltpu.VMEM(assign.shape, jnp.int32), pltpu.SemaphoreType.DMA((4,))],
        compiler_params=pltpu.CompilerParams(vmem_limit_bytes=12 << 20),
        cost_estimate=pl.CostEstimate(flops=0, bytes_accessed=size, transcendentals=0),
    )(assign, weight)


def split3(value):
    high = value.astype(BF16).astype(F32)
    mid = (value - high).astype(BF16).astype(F32)
    low = value - high - mid
    lane = iota((value.shape[0], LANES), 1)
    return jnp.where(
        lane == 0, high, jnp.where(lane == 1, mid, jnp.where(lane == 2, low, 0.0))
    ).astype(BF16)


def join3(value):
    return jnp.sum(value.astype(F32), axis=1, keepdims=True)


def project_tiles(scaled, weights, keep, send):
    half = keep.shape[0]
    for j, weight in enumerate(weights):
        width = weight.shape[1]
        for cols in tiles(width):
            product = jnp.dot(scaled[...], weight[:, cols], preferred_element_type=F32)
            at = slice(j * width + cols.start, j * width + cols.stop)
            keep[:, at] = product[:half]
            send[:, at] = product[half:].astype(BF16)


def first_body(share, rows, steps, order, first, second, gain, *refs):
    count = 1 + len(order)
    blocks, weights = refs[:count], refs[count:-4]
    blocks = [blocks[0]] + [blocks[1 + order.index(k)] for k in range(1, count)]
    scaled, keep, send, squares = refs[-4:]
    length, feats = blocks[0].shape
    total = first.shape[0]
    half, width = keep.shape
    for stage, picker in enumerate((first, second)):
        x = jnp.concatenate(
            [
                block[at : at + rows, :]
                for block in blocks
                for at in range(stage * rows, length, steps * rows)
            ]
        )
        sums = jnp.zeros((total, 1), F32)
        spots = [
            (slice(at, at + share), slice(at * steps + stage * share, at * steps + (stage + 1) * share))
            for at in range(0, total, share)
        ]
        for cols in tiles(feats):
            ordered = jnp.dot(picker[...], x[:, cols], preferred_element_type=F32)
            sums = sums + jnp.sum(ordered * ordered, axis=1, keepdims=True)
            value = (ordered * gain[:, cols]).astype(BF16)
            for source, target in spots:
                scaled[target, cols] = value[source]
        for source, target in spots:
            if target.start < half:
                squares[target, :] = jnp.broadcast_to(sums[source], (share, LANES))
            else:
                send[target.start - half : target.stop - half, width:] = split3(sums[source])
    project_tiles(scaled, weights, keep, send)


def next_body(scaled, *refs):
    *weights, keep, send = refs
    project_tiles(scaled, weights, keep, send)


def add_body(unit, with_squares, cuts, keep, got, *refs):
    width = keep.shape[1]
    if with_squares:
        squares, own, own_squares, *sends = refs
        total = squares[:, :1] + join3(got[:, width:])
        own_squares[...] = jnp.broadcast_to(total[:unit], own_squares.shape)
    else:
        own, *sends = refs
    piece = width // cuts
    for cols in tiles(piece):
        for cut in range(cuts):
            at = slice(cut * piece + cols.start, cut * piece + cols.stop)
            own[:, at] = keep[:unit, at] + got[:unit, at].astype(F32)
            for p, send in enumerate(sends[cut::cuts], 1):
                part = slice(p * unit, (p + 1) * unit)
                send[:, cols] = (keep[part, at] + got[part, at].astype(F32)).astype(BF16)
    if with_squares:
        for p, send in enumerate(sends, 1):
            send[:, width:] = split3(total[p * unit : (p + 1) * unit])


def past_body(n, share, assign, conv, *refs):
    pools, (older, newer) = refs[:n], refs[n:]
    mine = lax.axis_index("narrow")

    def one(row, carry):
        cand = assign[0, assign[1, mine * share + row]]
        rel = lax.div(cand, share) ^ mine
        spot = lax.rem(cand, share)
        for j in range(3):
            both = pools[0][spot, j].astype(F32)
            for k in range(1, n):
                both = jnp.where(rel == k, pools[k][spot, j].astype(F32), both)
            first = conv[0, j : j + 1, :]
            older[j, pl.ds(row, 1), :] = first * both[0:1] + conv[1, j : j + 1, :] * both[1:2]
            newer[j, pl.ds(row, 1), :] = first * both[1:2]
        return carry

    lax.fori_loop(0, share, one, 0)


def mix_body(share, peers, cut, conv, older, newer, squares, *refs):
    owns, gots, (gated, fresh) = refs[:3], refs[3:-2], refs[-2:]
    width = gated.shape[1]
    total = squares[:, :1]
    for got in gots[:peers]:
        total = total + join3(got[:, owns[0].shape[1] :])
    scale = lax.rsqrt(total / D + 1e-05)
    for cols in tiles(width):
        at = slice(cut * width + cols.start, cut * width + cols.stop)
        gate = None
        for j in range(3):
            new = owns[j][:, at]
            for got in gots[j * peers : (j + 1) * peers]:
                new = new + got[:, cols if j == 2 else at].astype(F32)
            new = (new * scale).astype(BF16)
            new0, new1 = new[:share], new[share:]
            fresh[j, 0, :, cols] = new0
            fresh[j, 1, :, cols] = new1
            new0, new1 = new0.astype(F32), new1.astype(F32)
            last = conv[2, j : j + 1, at]
            mixed0 = older[j, :, at] + last * new0
            mixed1 = newer[j, :, at] + conv[1, j : j + 1, at] * new0 + last * new1
            mixed = jnp.concatenate([mixed0, mixed1])
            gate = mixed if gate is None else gate * mixed
        gated[:, cols] = gate.astype(BF16)


def sorted_rows(share, rows, first, second, pieces):
    lined = []
    for stage, picker in enumerate((first, second)):
        part = slice(stage * share, (stage + 1) * share)
        every = jnp.concatenate([piece[part, :] for piece in pieces])
        lined.append(
            lax.dot_general(
                picker[...], every, (((0,), (0,)), ((), ())), preferred_element_type=F32
            ).astype(BF16)
        )
    blocks = range(0, first.shape[0], rows)
    return jnp.concatenate([part[at : at + rows] for at in blocks for part in lined])


def begin_body(share, rows, first, second, weight, *refs):
    *pieces, total = refs
    lined = sorted_rows(share, rows, first, second, pieces)
    for cols in tiles(weight.shape[1]):
        total[:, cols] = jnp.dot(
            lined, weight[: lined.shape[1], cols], preferred_element_type=F32
        )


def finish_body(n, share, rows, first, second, weight, *refs):
    pieces, refs = refs[:n], refs[n:]
    begun = weight.shape[0] > pieces[0].shape[1]
    before = refs[0] if begun else None
    own, *rest = refs[1:] if begun else refs
    lined = sorted_rows(share, rows, first, second, pieces)
    block = own.shape[0]
    for cols in tiles(weight.shape[1]):
        product = jnp.dot(lined, weight[weight.shape[0] - lined.shape[1] :, cols], preferred_element_type=F32)
        if before is not None:
            product = product + before[:, cols]
        own[:, cols] = product[:block].astype(own.dtype)
        for k, ref in enumerate(rest, 1):
            ref[:, cols] = product[k * block : (k + 1) * block].astype(BF16)


def shards(tokens, assign, state, norm_gain, in_weight, conv_weight, out_weight):
    n = lax.axis_size("narrow")
    wide = lax.axis_size("wide")
    steps, rows, feats = tokens.shape
    share = state.shape[0]
    chans = in_weight.shape[2]
    outs = out_weight.shape[1]
    direct = wide <= 4
    order = [k for k in (2, 3, 1) if k < wide]
    evens = [2 * k for k in range(n // 2)]
    total = n * share
    half = total // 2

    mine_tokens = tokens.reshape(steps * rows, feats)
    if direct:
        blocks = [mine_tokens] + [swap(mine_tokens, "wide", k) for k in order]
    else:
        blocks = [lax.all_gather(mine_tokens, "wide", axis=0, tiled=True)]

    past = state.transpose(0, 2, 1, 3)
    pools = [past] * n
    for k in evens:
        pools[k] = swap(past, "narrow", k) if k else past
        pools[k + 1] = swap(pools[k], "narrow", 1)

    *pickers, w0, w1, w2 = load(n, share, rows, direct, assign, in_weight.transpose(1, 0, 2))
    weights = [w0, w1, w2]
    older, newer = call(
        functools.partial(past_body, n, share),
        [struct(3, share, chans, dtype=F32)] * 2,
        [assign, conv_weight, *pools],
        scalars=1,
    )

    unit = steps * share
    cost = 2 * steps * total * feats * chans
    owns, gots = [], []
    for group in GROUPS:
        first = not owns
        width = chans * len(group)
        wider = width + LANES * first
        shapes = [struct(steps * half, width, dtype=F32), struct(steps * half, wider)]
        if first:
            scaled, keep, send, squares = call(
                functools.partial(first_body, share, rows, steps, order if direct else []),
                [struct(steps * total, feats), *shapes, struct(steps * half, LANES, dtype=F32)],
                [*pickers, norm_gain.reshape(1, feats), *blocks, *(weights[j] for j in group)],
                flops=cost * len(group),
            )
        else:
            keep, send = call(
                next_body,
                shapes,
                [scaled, *(weights[j] for j in group)],
                flops=cost * len(group),
            )
        cuts = 2 if len(owns) == 2 and chans % (2 * LANES) == 0 else 1
        extra = [squares] if first else []
        kept = [struct(unit, width, dtype=F32)] + [struct(unit, LANES, dtype=F32)] * len(extra)
        result = call(
            functools.partial(add_body, unit, first, cuts),
            kept + [struct(unit, wider // cuts)] * ((n // 2 - 1) * cuts),
            [keep, swap(send, "narrow", 1), *extra],
        )
        owns.append(result[0])
        if first:
            squares = result[1]
        leaving = result[len(kept) :]
        gots += [
            [swap(p, "narrow", k) for p, k in zip(leaving[cut::cuts], evens[1:])]
            for cut in range(cuts)
        ]
    fresh, near, far = [], [], []
    for cut in range(cuts):
        gated, part = call(
            functools.partial(mix_body, share, n // 2 - 1, cut),
            [struct(unit, chans // cuts), struct(3, 2, share, chans // cuts)],
            [conv_weight, older, newer, squares, *owns, *gots[0], *gots[1], *gots[2 + cut]],
        )
        fresh.append(part)
        near.append([swap(gated, "narrow", k) if k else gated for k in evens])
        far.append([swap(piece, "narrow", 1) for piece in near[-1]])
    fresh = jnp.concatenate(fresh, axis=3)
    block = steps * rows
    shapes = [struct(steps * total, outs)]
    if direct:
        shapes = [struct(block, outs, dtype=F32)] + [struct(block, outs)] * (wide - 1)
    cost = 2 * steps * total * (chans // cuts) * outs
    begun = []
    if cuts == 2:
        begun = call(
            functools.partial(begin_body, share, rows),
            [struct(steps * total, outs, dtype=F32)],
            [*pickers, out_weight, *near[0], *far[0]],
            flops=cost,
        )
    out, *parts = call(
        functools.partial(finish_body, n, share, rows),
        shapes,
        [*pickers, out_weight, *near[-1], *far[-1], *begun],
        flops=cost,
    )
    if direct:
        for k in [k for k in (2, 1, 3) if k < wide]:
            out = out + swap(parts[k - 1], "wide", k).astype(F32)
        out = out.astype(BF16)
    else:
        out = lax.psum_scatter(out, "wide", scatter_dimension=0, tiled=True)
    return (out.reshape(steps, rows, outs), fresh.transpose(2, 1, 0, 3))


def solution(mesh):
    in_specs = (
        P(None, ("groups", "wide"), "narrow"),
        P(None, "groups"),
        P(("groups", "narrow"), None, None, "wide"),
        P("narrow"),
        P("narrow", None, "wide"),
        P(None, None, "wide"),
        P("wide", "narrow"),
    )
    out_specs = (P(None, ("groups", "wide"), "narrow"), P(("groups", "narrow"), None, None, "wide"))
    return jax.shard_map(shards, mesh=mesh, in_specs=in_specs, out_specs=out_specs, check_vma=False)
```
